32 devices in a mesh: parts: 2 (over x), tensor: 16 (over z, y, core).
Axes of the slice: x: 2, y: 2, z: 4, core: 2. Of those that a mesh axis runs over, the one named last changes fastest.
Arguments:
- layer_input: bfloat16 [32768, 4096], P(('parts', 'tensor')), parts along dimension 0, may hold values from -6 to 6
- down_grad: bfloat16 [32768, 4096], P(('parts', 'tensor')), parts along dimension 0, may hold values from -6 to 6
- up_grad: bfloat16 [32768, 14336], P('parts', 'tensor'), parts along dimension 0, may hold values from -6 to 6
- hidden: bfloat16 [32768, 14336], P('parts', 'tensor'), parts along dimension 0, may hold values from -6 to 6
- proj_model: bfloat16 [4096, 128], replicated, may hold values from -0.09375 to 0.09375
- proj_hidden: bfloat16 [14336, 128], P('tensor'), may hold values from -1 to 1
- assignment: int32 [64], P('parts'), parts along dimension 0, may hold values from 0 to 31, each once
- query_bank: bfloat16 [512, 8192], P('parts', 'tensor'), parts along dimension 0, may hold values from -6 to 6
- query_ids: int32 [512], P('parts'), parts along dimension 0, may hold values from 0 to 255, each once
Outputs:
- sketches: float32 [64, 8192], P('parts', 'tensor'), parts along dimension 0
- scores: float32 [64, 256], P('parts', 'tensor'), parts along dimension 0
The draws below stay inside these ranges and needn't reach their ends.
There are 2 independent parts, one for each index of `parts`. The reference program is written for one: setup_inputs(seed, part) draws one part's arguments, and reference() takes and returns one part's arrays. A program takes and returns all parts, laid end to end along the dimension named above; an argument that names none is the same for every part. Nothing has to cross between parts.
Inputs may be any that keep to these rules, and one draw needn't show every extreme that they name: `assignment`: every document appears in exactly one slot. `query_ids`: every bank row appears in exactly one column.
All inputs are finite; a program needn't handle non-finite values.
Results may differ from the reference program's by a relative error of at most 0.008.
Values may be sent and summed in bfloat16 or wider, within the bound.
A program may use at most 192 MiB of HBM per device.

```python
import math
import jax
import jax.numpy as jnp
from jax import lax

D = 4096
FF = 14336
R = 64
SEQ = 512
EXAMPLES = 32
TOKENS = 16384
Q = 256


def draw_proj_hidden(key, part):
    key = jax.random.fold_in(key, 11)
    first, second, third = jax.random.split(key, 3)
    base = jnp.clip(jax.random.normal(first, (FF, 2 * R), jnp.float32), -6.0, 6.0)
    row_scale = jnp.exp(jax.random.uniform(second, (FF, 1), jnp.float32, math.log(1.0 / 3.0), math.log(3.0)))
    col_scale = jnp.exp(jax.random.uniform(third, (1, 2 * R), jnp.float32, 0.0, math.log(10.0))) / 4.0
    values = base * row_scale * col_scale / math.sqrt(FF)
    return jnp.clip(values, -1.0, 1.0).astype(jnp.bfloat16)


def block_levels(key, dims, shards, low, high):
    level, own = 1.0, jax.random.fold_in(key, 6)
    for axis_at, shards_of in shards:
        draws = jnp.exp(jax.random.uniform(jax.random.fold_in(own, axis_at), (shards_of,), jnp.float32, low / len(shards), high / len(shards)))
        level = level * jnp.repeat(draws, dims[axis_at] // shards_of).reshape([-1 if axis == axis_at else 1 for axis in range(len(dims))])
    return level


def normal_values(key, dims, width, most, cuts=(), dtype=jnp.bfloat16):
    factor_of = block_levels(key, dims, cuts, -0.22, 0.18) if cuts else 1.0
    values = jax.random.normal(key, dims, jnp.float32) * width * factor_of
    return jnp.minimum(jnp.maximum(values, -most), most).astype(dtype)


def setup_inputs(seed: int = 0, part: int = 0) -> dict:
    streams_of = jax.random.split(jax.random.key(seed), 10)
    part_splits = jax.random.split(jax.random.fold_in(streams_of[9], part), 10)
    layer_input = normal_values(part_splits[0], (TOKENS, D), 1.0, 6.0, ((0, 16),))
    down_grad = normal_values(part_splits[1], (TOKENS, D), 1.0, 6.0, ((0, 16),))
    up_grad = normal_values(part_splits[2], (TOKENS, FF), 1.0, 6.0, ((1, 16),))
    hidden = normal_values(part_splits[3], (TOKENS, FF), 1.0, 6.0, ((1, 16),))
    proj_model = normal_values(streams_of[4], (D, 2 * R), D ** -0.5, 0.09375)
    proj_hidden = draw_proj_hidden(jax.random.fold_in(streams_of[9], 71), part)
    assignment = jax.random.permutation(part_splits[6], EXAMPLES).astype(jnp.int32)
    query_bank = normal_values(part_splits[7], (Q, 2 * R * R), 1.0, 6.0, ((1, 16),))
    query_ids = jax.random.permutation(part_splits[8], Q).astype(jnp.int32)
    return {"layer_input": layer_input, "down_grad": down_grad, "up_grad": up_grad, "hidden": hidden, "proj_model": proj_model, "proj_hidden": proj_hidden, "assignment": assignment, "query_bank": query_bank, "query_ids": query_ids}


def normalize(slots, sketch_width):
    halves = slots.reshape(slots.shape[0], 2, sketch_width * sketch_width)
    inverse = lax.rsqrt(lax.optimization_barrier(jnp.mean(halves * halves, axis=2, keepdims=True)) + 1e-06)
    return (halves * inverse).reshape(slots.shape[0], 2 * sketch_width * sketch_width)

def blocks(matrix):
    return matrix.reshape(EXAMPLES, SEQ, matrix.shape[1])

def reference(layer_input, down_grad, up_grad, hidden, proj_model, proj_hidden, assignment, query_bank, query_ids):
    input_up = jnp.dot(layer_input, proj_model[:, :R], preferred_element_type=jnp.float32).astype(jnp.bfloat16)
    output_down = jnp.dot(down_grad, proj_model[:, R:], preferred_element_type=jnp.float32).astype(jnp.bfloat16)
    output_up = jnp.dot(up_grad, proj_hidden[:, :R], preferred_element_type=jnp.float32)
    input_down = jnp.dot(hidden, proj_hidden[:, R:], preferred_element_type=jnp.float32)
    up_part = jnp.einsum('etr,ets->ers', blocks(output_up), blocks(input_up).astype(jnp.float32))
    down_part = jnp.einsum('etr,ets->ers', blocks(output_down).astype(jnp.float32), blocks(input_down))
    documents = jnp.concatenate([up_part.reshape(EXAMPLES, R * R), down_part.reshape(EXAMPLES, R * R)], axis=1)
    slots = jnp.take(documents, assignment.astype(jnp.int32), axis=0)
    sketches = normalize(slots, R)
    rounded = sketches.astype(jnp.bfloat16)
    score_scale = 1.0 / math.sqrt(2 * R * R)
    bank_scores = jnp.dot(rounded, query_bank.T, preferred_element_type=jnp.float32) * score_scale
    scores = jnp.take(bank_scores, query_ids.astype(jnp.int32), axis=1)
    return (sketches, scores)
```

```python
import math

import jax
import jax.numpy as jnp
from jax import lax
from jax.experimental import pallas as pl
from jax.experimental.pallas import tpu as pltpu
from jax.sharding import PartitionSpec as P

SEQ = 512


def blocks(matrix):
    return matrix.reshape(matrix.shape[0] // SEQ, SEQ, matrix.shape[1])


def on_device(
    layer_input,
    down_grad,
    up_grad,
    hidden,
    proj_model,
    proj_hidden,
    assignment,
    query_bank,
    query_ids,
):
    sketch_width = proj_model.shape[1] // 2
    count_docs = up_grad.shape[0] // SEQ
    columns = query_bank.shape[1]
    device = lax.axis_index("tensor")
    local_up = jnp.dot(
        layer_input, proj_model[:, :sketch_width], preferred_element_type=jnp.float32
    ).astype(jnp.bfloat16)
    local_down = jnp.dot(
        down_grad, proj_model[:, sketch_width:], preferred_element_type=jnp.float32
    ).astype(jnp.bfloat16)
    every_up, every_down = (
        lax.all_gather(local_up, "tensor", axis=0, tiled=True),
        lax.all_gather(local_down, "tensor", axis=0, tiled=True),
    )
    output_up = jnp.dot(up_grad, proj_hidden[:, :sketch_width], preferred_element_type=jnp.float32)
    input_down = jnp.dot(hidden, proj_hidden[:, sketch_width:], preferred_element_type=jnp.float32)
    up_part = jnp.einsum("etr,ets->rse", blocks(output_up), blocks(every_up).astype(jnp.float32))
    down_part = jnp.einsum(
        "etr,ets->rse", blocks(every_down).astype(jnp.float32), blocks(input_down)
    )
    entry_terms = jnp.concatenate(
        [up_part.reshape(-1, count_docs), down_part.reshape(-1, count_docs)], axis=0
    )
    summed = lax.psum_scatter(entry_terms, "tensor", scatter_dimension=0, tiled=True)
    slots = jnp.take(summed, assignment, axis=1).T
    which_half = device * columns // (sketch_width * sketch_width)
    half_mask = (jnp.arange(2) == which_half).astype(jnp.float32)
    squares = jnp.sum(slots * slots, axis=1)
    totals = lax.psum(squares[:, None] * half_mask[None, :], "tensor")
    inverse = lax.rsqrt(totals / (sketch_width * sketch_width) + 1e-06)
    own_inverse = jnp.sum(inverse * half_mask[None, :], axis=1)
    sketches = slots * own_inverse[:, None]
    rounded = sketches.astype(jnp.bfloat16)
    partial_scores = jnp.dot(rounded, query_bank.T, preferred_element_type=jnp.float32)
    score_scale = 1.0 / math.sqrt(2 * sketch_width * sketch_width)
    own_columns = query_ids.shape[0] // lax.axis_size("tensor")
    bank_scores = lax.psum(partial_scores, "tensor")
    own_ids = lax.dynamic_slice_in_dim(query_ids, device * own_columns, own_columns, 0)
    raw_scores = jnp.take(bank_scores, own_ids, axis=1)
    scores = raw_scores * score_scale
    return (sketches, scores)


AXIS = "tensor"
RING = 8
F32 = jnp.float32
BF16 = jnp.bfloat16
HIGH = lax.Precision.HIGHEST


def lanes(shape):
    return lax.broadcasted_iota(jnp.int32, shape, len(shape) - 1)


def rows(shape):
    return lax.broadcasted_iota(jnp.int32, shape, len(shape) - 2)


def fused_kernel(
    layer_ref, down_ref, up_ref, hidden_ref, model_ref, proj_ref, assign_ref, bank_ref, ids_ref,
    sketches_ref, scores_ref,
    layer_buf, down_buf, stream, factors, weights, placed_bank, pick, staged, partials, share, shares,
    load_sem, stream_sem, factor_send, factor_recv, sketch_send, sketch_recv, share_send, share_recv,
):
    me = lax.axis_index(AXIS)
    core = me % 2
    row_y = (me // 2) % 2
    row_z = me // 4
    far = row_z // 2
    near_z = row_z + far * (3 - 2 * row_z)
    sibling = me + 1 - 2 * core
    across = me + 2 - 4 * row_y
    width = up_ref.shape[1]

    barrier = pltpu.get_barrier_semaphore()

    @pl.loop(1, 16)
    def _(step):
        pl.semaphore_signal(
            barrier, inc=1, device_id={AXIS: (me + step) % 16}, device_id_type=pl.DeviceIdType.MESH
        )

    def chip_of(group):
        p = group // 2
        near = jnp.where(p < 2, (p + near_z) % 2, p)
        source_z = near + far * (3 - 2 * near)
        source_y = (row_y + group % 2) % 2
        return source_z * 2 + source_y

    def doc_of(group, u):
        return (chip_of(group) * 2 + (core + u // 2) % 2) * 2 + u % 2

    def loads(chunk):
        at = pl.ds(chunk * 256, 256)
        return (
            pltpu.make_async_copy(layer_ref.at[at], layer_buf.at[at], load_sem.at[chunk, 0]),
            pltpu.make_async_copy(down_ref.at[at], down_buf.at[at], load_sem.at[chunk, 1]),
        )

    def streams(group, u):
        at = pl.ds(pl.multiple_of(doc_of(group, u) * SEQ, SEQ), SEQ)
        slot = (group % (RING // 4)) * 4 + u
        return (
            pltpu.make_async_copy(
                up_ref.at[at], stream.at[slot, :, pl.ds(0, width)], stream_sem.at[slot, 0]
            ),
            pltpu.make_async_copy(
                hidden_ref.at[at], stream.at[slot, :, pl.ds(width, width)], stream_sem.at[slot, 1]
            ),
        )

    def send_doc(doc, target):
        pltpu.make_async_remote_copy(
            src_ref=factors.at[doc],
            dst_ref=factors.at[doc],
            send_sem=factor_send,
            recv_sem=factor_recv.at[doc],
            device_id={AXIS: target},
            device_id_type=pl.DeviceIdType.MESH,
        ).start()

    for chunk in range(4):
        for copy in loads(chunk):
            copy.start()
    for group in range(RING // 4):
        for u in range(4):
            for copy in streams(group, u):
                copy.start()

    proj = proj_ref[...]
    left = lanes(proj.shape) < 64
    weights[0:width, :] = jnp.where(left, proj, jnp.zeros_like(proj))
    weights[width : 2 * width, :] = jnp.where(left, jnp.zeros_like(proj), proj)

    left256 = lanes((256, 128)) < 64
    for chunk in range(4):
        for copy in loads(chunk):
            copy.wait()
        at = pl.ds(chunk * 256, 256)
        ups = jnp.dot(layer_buf[at, :], model_ref[...], preferred_element_type=F32)
        downs = jnp.dot(down_buf[at, :], model_ref[...], preferred_element_type=F32)
        doc = me * 2 + chunk // 2
        factors[doc, pl.ds((chunk % 2) * 256, 256), :] = jnp.where(left256, ups, downs).astype(BF16)
        if chunk == 1:
            pl.semaphore_wait(barrier, 15)
        if chunk % 2 == 1:
            send_doc(doc, across)
            send_doc(doc, sibling)
            for hop in range(1, 4):
                near = jnp.where(hop < 2, (hop + near_z) % 2, hop)
                other_z = near + far * (3 - 2 * near)
                send_doc(doc, other_z * 4 + row_y * 2 + core)

    ids = ids_ref[...]
    matches = (rows((256, 256)) == ids).astype(BF16)
    placed_bank[...] = lax.dot_general(
        matches, bank_ref[...], (((0,), (0,)), ((), ())), preferred_element_type=F32
    ).astype(BF16)

    row_at = rows((256, 128))
    wanted = jnp.zeros((256, 128), jnp.int32)
    for slot in range(32):
        wanted = jnp.where(row_at % 32 == slot, assign_ref[slot], wanted)
    lane_at = lanes((256, 128))
    same_row = lane_at % 8 == row_at // 32
    for d in range(2):
        hit = jnp.logical_and(same_row, wanted == (lane_at // 8) * 2 + d)
        pick[d] = hit.astype(F32)

    def pass_on(group, u):
        doc = doc_of(group, u)
        pltpu.make_async_copy(factors.at[doc], factors.at[doc], factor_recv.at[doc]).wait()
        if u < 2:
            send_doc(doc, sibling)

            @pl.when(group % 2 == 0)
            def _():
                send_doc(doc, across)

    pass_on(0, 2)
    pass_on(0, 3)

    left512 = lanes((SEQ, 128)) < 64
    left64 = lanes((64, 128)) < 64

    @pl.loop(0, 8)
    def _(group):
        sums = []
        for u in range(4):
            for copy in streams(group, u):
                copy.wait()
            slot = (group % (RING // 4)) * 4 + u
            hidden_side = jnp.dot(stream[slot], weights[...], preferred_element_type=F32).astype(BF16)
            model_side = factors[doc_of(group, u)]
            outer = jnp.where(left512, hidden_side, model_side)
            inner = jnp.where(left512, model_side, hidden_side)
            sums.append(
                lax.dot_general(outer, inner, (((0,), (0,)), ((), ())), preferred_element_type=F32)
            )

            @pl.when(group < 8 - RING // 4)
            def _():
                for copy in streams(group + RING // 4, u):
                    copy.start()

            @pl.when(group < 7)
            def _():
                pass_on(group + 1, u)

        packed = []
        for c in range(2):
            first, second = sums[2 * c], sums[2 * c + 1]
            upper = jnp.where(left64, first[:64], pltpu.roll(second[:64], 64, 1))
            lower = jnp.where(left64, pltpu.roll(first[64:], 64, 1), second[64:])
            packed.append(jnp.concatenate([upper, lower], axis=0))
        even = core == 0
        first = jnp.where(even, packed[0], packed[1]).reshape(16, 8, 128)
        second = jnp.where(even, packed[1], packed[0]).reshape(16, 8, 128)
        staged[group] = jnp.concatenate([first, second], axis=1).astype(BF16)
        chip = chip_of(group)

        @pl.loop(1, 16)
        def _(step):
            target = (me + step) % 16
            pltpu.make_async_remote_copy(
                src_ref=staged.at[group, target],
                dst_ref=partials.at[me, chip],
                send_sem=sketch_send,
                recv_sem=sketch_recv,
                device_id={AXIS: target},
                device_id_type=pl.DeviceIdType.MESH,
            ).start()

        partials[me, chip] = staged[group, me]

    most = partials.at[pl.ds(0, 15)]
    pltpu.make_async_copy(most, most, sketch_recv).wait()
    total = partials[0].astype(F32)
    for sender in range(1, 16):
        total = total + partials[sender].astype(F32)
    total = total.reshape(128, 128)
    picked = [
        jnp.dot(pick[d], total, preferred_element_type=F32, precision=HIGH) for d in range(2)
    ]
    left32 = lanes((32, 128)) < 64
    tiles = []
    for pair in range(4):
        a0, a1 = (picked[d][pair * 64 : pair * 64 + 32] for d in range(2))
        b0, b1 = (picked[d][pair * 64 + 32 : pair * 64 + 64] for d in range(2))
        tiles.append(
            jnp.where(left32, a0 + pltpu.roll(a1, 64, 1), pltpu.roll(b0, 64, 1) + b1)
        )
    slots = jnp.concatenate(tiles, axis=1)
    nothing = jnp.zeros((32, slots.shape[1]), F32)
    across_rows = (((1,), (1,)), ((), ()))
    padded = jnp.concatenate([slots, nothing, nothing, nothing], axis=0).astype(BF16)
    raw = lax.dot_general(placed_bank[...], padded, across_rows, preferred_element_type=F32)
    squares = jnp.concatenate([nothing, nothing, slots * slots, nothing], axis=0)
    norms = lax.dot_general(
        jnp.ones((8, slots.shape[1]), F32), squares, across_rows,
        preferred_element_type=F32, precision=HIGH,
    )
    raw = raw.reshape(16, 2, 8, 128)
    second = pltpu.roll(raw[:, 1].reshape(128, 128), 32, 1).reshape(16, 8, 128)
    share[...] = raw[:, 0] + second + norms[None]

    @pl.loop(1, 16)
    def _(step):
        target = (me + step) % 16
        pltpu.make_async_remote_copy(
            src_ref=share.at[target],
            dst_ref=shares.at[me],
            send_sem=share_send,
            recv_sem=share_recv,
            device_id={AXIS: target},
            device_id_type=pl.DeviceIdType.MESH,
        ).start()

    shares[me] = share[me]
    most = factors.at[pl.ds(0, 30)]
    pltpu.make_async_copy(most, most, factor_send).wait()
    most = partials.at[pl.ds(0, 15)]
    pltpu.make_async_copy(most, most, sketch_send).wait()
    most = shares.at[pl.ds(0, 15)]
    pltpu.make_async_copy(most, most, share_recv).wait()
    halves = [jnp.sum(shares[8 * h : 8 * h + 8], axis=0) for h in range(2)]
    inverses = [lax.rsqrt(half * (1.0 / 4096) + 1e-06) for half in halves]
    lane8 = lanes((8, 128))
    own = jnp.where(me >= 8, inverses[1], inverses[0])
    first_row = (rows((8, 128)) == 0).astype(F32)
    over_rows = (((0,), (0,)), ((), ()))
    spread = lax.dot_general(
        own, first_row, over_rows, preferred_element_type=F32, precision=HIGH
    )[64:96]
    for tile in range(4):
        sketches_ref[:, 128 * tile : 128 * tile + 128] = tiles[tile] * spread
    scaled = jnp.zeros((8, 128), F32)
    for half, inverse in zip(halves, inverses):
        moved = jnp.where(lane8 < 32, pltpu.roll(inverse, 64, 1), pltpu.roll(inverse, 96, 1))
        scaled = scaled + half * moved
    scaled = jnp.where(lane8 < 64, scaled * (1.0 / math.sqrt(8192)), 0.0)
    out = jnp.zeros((32, 128), F32)
    for b in range(2):
        place = (lane8 == rows((8, 128)) + 8 * b).astype(F32)
        turned = lax.dot_general(
            scaled, place, over_rows, preferred_element_type=F32, precision=HIGH
        )
        out = out + turned[32 * b : 32 * b + 32]
    scores_ref[...] = out[:, :16]
    most = share.at[pl.ds(0, 15)]
    pltpu.make_async_copy(most, most, share_send).wait()


def fused(
    layer_input, down_grad, up_grad, hidden, proj_model, proj_hidden, assignment, query_bank, query_ids
):
    vmem = pl.BlockSpec(memory_space=pltpu.VMEM)
    smem = pl.BlockSpec(memory_space=pltpu.SMEM)
    hbm = pl.BlockSpec(memory_space=pl.ANY)
    width = up_grad.shape[1]
    return pl.pallas_call(
        fused_kernel,
        out_shape=(
            jax.ShapeDtypeStruct((32, 512), F32),
            jax.ShapeDtypeStruct((32, 16), F32),
        ),
        in_specs=[hbm, hbm, hbm, hbm, vmem, vmem, smem, vmem, vmem],
        out_specs=(vmem, vmem),
        scratch_shapes=[
            pltpu.VMEM(layer_input.shape, BF16),
            pltpu.VMEM(down_grad.shape, BF16),
            pltpu.VMEM((RING, SEQ, 2 * width), BF16),
            pltpu.VMEM((32, SEQ, 128), BF16),
            pltpu.VMEM((2 * width, 128), BF16),
            pltpu.VMEM((256, 512), BF16),
            pltpu.VMEM((2, 256, 128), F32),
            pltpu.VMEM((8, 16, 16, 128), BF16),
            pltpu.VMEM((16, 8, 16, 128), BF16),
            pltpu.VMEM((16, 8, 128), F32),
            pltpu.VMEM((16, 8, 128), F32),
            pltpu.SemaphoreType.DMA((4, 2)),
            pltpu.SemaphoreType.DMA((RING, 2)),
            pltpu.SemaphoreType.DMA,
            pltpu.SemaphoreType.DMA((32,)),
            pltpu.SemaphoreType.DMA,
            pltpu.SemaphoreType.DMA,
            pltpu.SemaphoreType.DMA,
            pltpu.SemaphoreType.DMA,
        ],
        compiler_params=pltpu.CompilerParams(
            collective_id=0, has_side_effects=True, vmem_limit_bytes=56 * 1024 * 1024
        ),
    )(
        layer_input, down_grad, up_grad, hidden, proj_model, proj_hidden,
        assignment, query_bank, query_ids.reshape(1, -1),
    )


def choose(*arrays):
    shapes = tuple(array.shape for array in arrays)
    fits = (
        (1024, 4096), (1024, 4096), (16384, 896), (16384, 896), (4096, 128), (896, 128),
        (32,), (256, 512), (256,),
    )
    if lax.axis_size(AXIS) == 16 and shapes == fits:
        return fused(*arrays)
    return on_device(*arrays)


def solution(mesh):
    placed = (
        P(("parts", "tensor"), None),
        P(("parts", "tensor"), None),
        P("parts", "tensor"),
        P("parts", "tensor"),
        P(),
        P("tensor", None),
        P("parts"),
        P("parts", "tensor"),
        P("parts"),
    )
    return jax.shard_map(
        choose,
        mesh=mesh,
        in_specs=placed,
        out_specs=(P("parts", "tensor"), P("parts", "tensor")),
        check_vma=False,
    )
```

```python
import math

import jax
import jax.numpy as jnp
from jax import lax
from jax.experimental import pallas as pl
from jax.experimental.pallas import tpu as pltpu
from jax.sharding import PartitionSpec as P

SEQ = 512


def blocks(matrix):
    return matrix.reshape(matrix.shape[0] // SEQ, SEQ, matrix.shape[1])


def on_device(
    layer_input,
    down_grad,
    up_grad,
    hidden,
    proj_model,
    proj_hidden,
    assignment,
    query_bank,
    query_ids,
):
    sketch_width = proj_model.shape[1] // 2
    count_docs = up_grad.shape[0] // SEQ
    columns = query_bank.shape[1]
    device = lax.axis_index("tensor")
    local_up = jnp.dot(
        layer_input, proj_model[:, :sketch_width], preferred_element_type=jnp.float32
    ).astype(jnp.bfloat16)
    local_down = jnp.dot(
        down_grad, proj_model[:, sketch_width:], preferred_element_type=jnp.float32
    ).astype(jnp.bfloat16)
    every_up, every_down = (
        lax.all_gather(local_up, "tensor", axis=0, tiled=True),
        lax.all_gather(local_down, "tensor", axis=0, tiled=True),
    )
    output_up = jnp.dot(up_grad, proj_hidden[:, :sketch_width], preferred_element_type=jnp.float32)
    input_down = jnp.dot(hidden, proj_hidden[:, sketch_width:], preferred_element_type=jnp.float32)
    up_part = jnp.einsum("etr,ets->rse", blocks(output_up), blocks(every_up).astype(jnp.float32))
    down_part = jnp.einsum(
        "etr,ets->rse", blocks(every_down).astype(jnp.float32), blocks(input_down)
    )
    entry_terms = jnp.concatenate(
        [up_part.reshape(-1, count_docs), down_part.reshape(-1, count_docs)], axis=0
    )
    summed = lax.psum_scatter(entry_terms, "tensor", scatter_dimension=0, tiled=True)
    slots = jnp.take(summed, assignment, axis=1).T
    which_half = device * columns // (sketch_width * sketch_width)
    half_mask = (jnp.arange(2) == which_half).astype(jnp.float32)
    squares = jnp.sum(slots * slots, axis=1)
    totals = lax.psum(squares[:, None] * half_mask[None, :], "tensor")
    inverse = lax.rsqrt(totals / (sketch_width * sketch_width) + 1e-06)
    own_inverse = jnp.sum(inverse * half_mask[None, :], axis=1)
    sketches = slots * own_inverse[:, None]
    rounded = sketches.astype(jnp.bfloat16)
    partial_scores = jnp.dot(rounded, query_bank.T, preferred_element_type=jnp.float32)
    score_scale = 1.0 / math.sqrt(2 * sketch_width * sketch_width)
    own_columns = query_ids.shape[0] // lax.axis_size("tensor")
    bank_scores = lax.psum(partial_scores, "tensor")
    own_ids = lax.dynamic_slice_in_dim(query_ids, device * own_columns, own_columns, 0)
    raw_scores = jnp.take(bank_scores, own_ids, axis=1)
    scores = raw_scores * score_scale
    return (sketches, scores)


AXIS = "tensor"
RING = 8
UNIT = 4
F32 = jnp.float32
BF16 = jnp.bfloat16
HIGH = lax.Precision.HIGHEST


def lanes(shape):
    return lax.broadcasted_iota(jnp.int32, shape, len(shape) - 1)


def rows(shape):
    return lax.broadcasted_iota(jnp.int32, shape, len(shape) - 2)


def fused_kernel(
    layer_ref, down_ref, up_ref, hidden_ref, model_ref, proj_ref, assign_ref, bank_ref, ids_ref,
    sketches_ref, scores_ref,
    layer_buf, down_buf, stream, factors, weights, placed_bank, pick, staged, partials, share, shares,
    load_sem, stream_sem, factor_send, factor_recv, sketch_send, sketch_recv, share_send, share_recv,
):
    me = lax.axis_index(AXIS)
    core = me % 2
    row_y = (me // 2) % 2
    row_z = me // 4
    far = row_z // 2
    near_z = row_z + far * (3 - 2 * row_z)
    sibling = me + 1 - 2 * core
    across = me + 2 - 4 * row_y
    width = up_ref.shape[1]

    barrier = pltpu.get_barrier_semaphore()

    @pl.loop(1, 16)
    def _(step):
        pl.semaphore_signal(
            barrier, inc=1, device_id={AXIS: (me + step) % 16}, device_id_type=pl.DeviceIdType.MESH
        )

    def chip_of(group):
        p = group // 2
        near = jnp.where(p < 2, (p + near_z) % 2, p)
        source_z = near + far * (3 - 2 * near)
        source_y = (row_y + group % 2) % 2
        return source_z * 2 + source_y

    def doc_of(group, u):
        return (chip_of(group) * 2 + (core + u // 2) % 2) * 2 + u % 2

    def loads(chunk):
        at = pl.ds(chunk * SEQ, SEQ)
        return (
            pltpu.make_async_copy(layer_ref.at[at], layer_buf.at[at], load_sem.at[chunk, 0]),
            pltpu.make_async_copy(down_ref.at[at], down_buf.at[at], load_sem.at[chunk, 1]),
        )

    def slot_rows(group, u, count):
        first = ((group % (RING // 4)) * 4 + u) * SEQ
        return pl.ds(pl.multiple_of(first, SEQ), count * SEQ)

    def streams(group, u):
        at = pl.ds(pl.multiple_of(doc_of(group, u) * SEQ, SEQ), SEQ)
        slot = (group % (RING // 4)) * 4 + u
        return (
            pltpu.make_async_copy(
                up_ref.at[at], stream.at[slot_rows(group, u, 1), pl.ds(0, width)], stream_sem.at[slot, 0]
            ),
            pltpu.make_async_copy(
                hidden_ref.at[at], stream.at[slot_rows(group, u, 1), pl.ds(width, width)], stream_sem.at[slot, 1]
            ),
        )

    def send_doc(doc, target):
        pltpu.make_async_remote_copy(
            src_ref=factors.at[doc],
            dst_ref=factors.at[doc],
            send_sem=factor_send,
            recv_sem=factor_recv.at[doc],
            device_id={AXIS: target},
            device_id_type=pl.DeviceIdType.MESH,
        ).start()

    for chunk in range(2):
        for copy in loads(chunk):
            copy.start()
    for group in range(RING // 4):
        for u in range(4):
            for copy in streams(group, u):
                copy.start()

    proj = proj_ref[...]
    left = lanes(proj.shape) < 64
    weights[0:width, :] = jnp.where(left, proj, jnp.zeros_like(proj))
    weights[width : 2 * width, :] = jnp.where(left, jnp.zeros_like(proj), proj)

    left512 = lanes((SEQ, 128)) < 64
    for chunk in range(2):
        for copy in loads(chunk):
            copy.wait()
        at = pl.ds(chunk * SEQ, SEQ)
        ups = jnp.dot(layer_buf[at, :], model_ref[...], preferred_element_type=F32)
        downs = jnp.dot(down_buf[at, :], model_ref[...], preferred_element_type=F32)
        doc = me * 2 + chunk
        factors[doc] = jnp.where(left512, ups, downs).astype(BF16)
        if chunk == 0:
            pl.semaphore_wait(barrier, 15)
        send_doc(doc, across)
        send_doc(doc, sibling)
        for hop in range(1, 4):
            near = jnp.where(hop < 2, (hop + near_z) % 2, hop)
            other_z = near + far * (3 - 2 * near)
            send_doc(doc, other_z * 4 + row_y * 2 + core)

    ids = ids_ref[...]
    matches = (rows((256, 256)) == ids).astype(BF16)
    placed_bank[...] = lax.dot_general(
        matches, bank_ref[...], (((0,), (0,)), ((), ())), preferred_element_type=F32
    ).astype(BF16)

    row_at = rows((256, 128))
    wanted = jnp.zeros((256, 128), jnp.int32)
    for slot in range(32):
        wanted = jnp.where(row_at % 32 == slot, assign_ref[slot], wanted)
    lane_at = lanes((256, 128))
    same_row = lane_at % 8 == row_at // 32
    for d in range(2):
        hit = jnp.logical_and(same_row, wanted == (lane_at // 8) * 2 + d)
        pick[d] = hit.astype(F32)

    def pass_on(group, u):
        doc = doc_of(group, u)
        pltpu.make_async_copy(factors.at[doc], factors.at[doc], factor_recv.at[doc]).wait()
        if u < 2:
            send_doc(doc, sibling)

            @pl.when(group % 2 == 0)
            def _():
                send_doc(doc, across)

    pass_on(0, 2)
    pass_on(0, 3)

    left64 = lanes((64, 128)) < 64

    @pl.loop(0, 8)
    def _(group):
        sums = []
        for base in range(0, 4, UNIT):
            for u in range(base, base + UNIT):
                for copy in streams(group, u):
                    copy.wait()
            hidden_sides = jnp.dot(
                stream[slot_rows(group, base, UNIT), :], weights[...], preferred_element_type=F32
            ).astype(BF16)
            for u in range(base, base + UNIT):
                hidden_side = hidden_sides[(u - base) * SEQ : (u - base + 1) * SEQ]
                model_side = factors[doc_of(group, u)]
                outer = jnp.where(left512, hidden_side, model_side)
                inner = jnp.where(left512, model_side, hidden_side)
                sums.append(
                    lax.dot_general(outer, inner, (((0,), (0,)), ((), ())), preferred_element_type=F32)
                )

            @pl.when(group < 8 - RING // 4)
            def _():
                for u in range(base, base + UNIT):
                    for copy in streams(group + RING // 4, u):
                        copy.start()

            @pl.when(group < 7)
            def _():
                for u in range(base, base + UNIT):
                    pass_on(group + 1, u)

        packed = []
        for c in range(2):
            first, second = sums[2 * c], sums[2 * c + 1]
            upper = jnp.where(left64, first[:64], pltpu.roll(second[:64], 64, 1))
            lower = jnp.where(left64, pltpu.roll(first[64:], 64, 1), second[64:])
            packed.append(jnp.concatenate([upper, lower], axis=0))
        even = core == 0
        first = jnp.where(even, packed[0], packed[1]).reshape(16, 8, 128)
        second = jnp.where(even, packed[1], packed[0]).reshape(16, 8, 128)
        staged[group] = jnp.concatenate([first, second], axis=1).astype(BF16)
        chip = chip_of(group)

        @pl.loop(1, 16)
        def _(step):
            target = (me + step) % 16
            pltpu.make_async_remote_copy(
                src_ref=staged.at[group, target],
                dst_ref=partials.at[me, chip],
                send_sem=sketch_send,
                recv_sem=sketch_recv,
                device_id={AXIS: target},
                device_id_type=pl.DeviceIdType.MESH,
            ).start()

        partials[me, chip] = staged[group, me]

    most = partials.at[pl.ds(0, 15)]
    pltpu.make_async_copy(most, most, sketch_recv).wait()
    total = partials[0].astype(F32)
    for sender in range(1, 16):
        total = total + partials[sender].astype(F32)
    total = total.reshape(128, 128)
    picked = [
        jnp.dot(pick[d], total, preferred_element_type=F32, precision=HIGH) for d in range(2)
    ]
    left32 = lanes((32, 128)) < 64
    tiles = []
    for pair in range(4):
        a0, a1 = (picked[d][pair * 64 : pair * 64 + 32] for d in range(2))
        b0, b1 = (picked[d][pair * 64 + 32 : pair * 64 + 64] for d in range(2))
        tiles.append(
            jnp.where(left32, a0 + pltpu.roll(a1, 64, 1), pltpu.roll(b0, 64, 1) + b1)
        )
    slots = jnp.concatenate(tiles, axis=1)
    nothing = jnp.zeros((32, slots.shape[1]), F32)
    across_rows = (((1,), (1,)), ((), ()))
    padded = jnp.concatenate([slots, nothing, nothing, nothing], axis=0).astype(BF16)
    raw = lax.dot_general(placed_bank[...], padded, across_rows, preferred_element_type=F32)
    squares = jnp.concatenate([nothing, nothing, slots * slots, nothing], axis=0)
    norms = lax.dot_general(
        jnp.ones((8, slots.shape[1]), F32), squares, across_rows,
        preferred_element_type=F32, precision=HIGH,
    )
    raw = raw.reshape(16, 2, 8, 128)
    second = pltpu.roll(raw[:, 1].reshape(128, 128), 32, 1).reshape(16, 8, 128)
    share[...] = raw[:, 0] + second + norms[None]

    @pl.loop(1, 16)
    def _(step):
        target = (me + step) % 16
        pltpu.make_async_remote_copy(
            src_ref=share.at[target],
            dst_ref=shares.at[me],
            send_sem=share_send,
            recv_sem=share_recv,
            device_id={AXIS: target},
            device_id_type=pl.DeviceIdType.MESH,
        ).start()

    shares[me] = share[me]
    most = factors.at[pl.ds(0, 30)]
    pltpu.make_async_copy(most, most, factor_send).wait()
    most = partials.at[pl.ds(0, 15)]
    pltpu.make_async_copy(most, most, sketch_send).wait()
    most = shares.at[pl.ds(0, 15)]
    pltpu.make_async_copy(most, most, share_recv).wait()
    halves = [jnp.sum(shares[8 * h : 8 * h + 8], axis=0) for h in range(2)]
    inverses = [lax.rsqrt(half * (1.0 / 4096) + 1e-06) for half in halves]
    lane8 = lanes((8, 128))
    own = jnp.where(me >= 8, inverses[1], inverses[0])
    first_row = (rows((8, 128)) == 0).astype(F32)
    over_rows = (((0,), (0,)), ((), ()))
    spread = lax.dot_general(
        own, first_row, over_rows, preferred_element_type=F32, precision=HIGH
    )[64:96]
    for tile in range(4):
        sketches_ref[:, 128 * tile : 128 * tile + 128] = tiles[tile] * spread
    scaled = jnp.zeros((8, 128), F32)
    for half, inverse in zip(halves, inverses):
        moved = jnp.where(lane8 < 32, pltpu.roll(inverse, 64, 1), pltpu.roll(inverse, 96, 1))
        scaled = scaled + half * moved
    scaled = jnp.where(lane8 < 64, scaled * (1.0 / math.sqrt(8192)), 0.0)
    out = jnp.zeros((32, 128), F32)
    for b in range(2):
        place = (lane8 == rows((8, 128)) + 8 * b).astype(F32)
        turned = lax.dot_general(
            scaled, place, over_rows, preferred_element_type=F32, precision=HIGH
        )
        out = out + turned[32 * b : 32 * b + 32]
    scores_ref[...] = out[:, :16]
    most = share.at[pl.ds(0, 15)]
    pltpu.make_async_copy(most, most, share_send).wait()


def fused(
    layer_input, down_grad, up_grad, hidden, proj_model, proj_hidden, assignment, query_bank, query_ids
):
    vmem = pl.BlockSpec(memory_space=pltpu.VMEM)
    smem = pl.BlockSpec(memory_space=pltpu.SMEM)
    hbm = pl.BlockSpec(memory_space=pl.ANY)
    width = up_grad.shape[1]
    return pl.pallas_call(
        fused_kernel,
        out_shape=(
            jax.ShapeDtypeStruct((32, 512), F32),
            jax.ShapeDtypeStruct((32, 16), F32),
        ),
        in_specs=[hbm, hbm, hbm, hbm, vmem, vmem, smem, vmem, vmem],
        out_specs=(vmem, vmem),
        scratch_shapes=[
            pltpu.VMEM(layer_input.shape, BF16),
            pltpu.VMEM(down_grad.shape, BF16),
            pltpu.VMEM((RING * SEQ, 2 * width), BF16),
            pltpu.VMEM((32, SEQ, 128), BF16),
            pltpu.VMEM((2 * width, 128), BF16),
            pltpu.VMEM((256, 512), BF16),
            pltpu.VMEM((2, 256, 128), F32),
            pltpu.VMEM((8, 16, 16, 128), BF16),
            pltpu.VMEM((16, 8, 16, 128), BF16),
            pltpu.VMEM((16, 8, 128), F32),
            pltpu.VMEM((16, 8, 128), F32),
            pltpu.SemaphoreType.DMA((2, 2)),
            pltpu.SemaphoreType.DMA((RING, 2)),
            pltpu.SemaphoreType.DMA,
            pltpu.SemaphoreType.DMA((32,)),
            pltpu.SemaphoreType.DMA,
            pltpu.SemaphoreType.DMA,
            pltpu.SemaphoreType.DMA,
            pltpu.SemaphoreType.DMA,
        ],
        compiler_params=pltpu.CompilerParams(
            collective_id=0, has_side_effects=True, vmem_limit_bytes=56 * 1024 * 1024
        ),
    )(
        layer_input, down_grad, up_grad, hidden, proj_model, proj_hidden,
        assignment, query_bank, query_ids.reshape(1, -1),
    )


def choose(*arrays):
    shapes = tuple(array.shape for array in arrays)
    fits = (
        (1024, 4096), (1024, 4096), (16384, 896), (16384, 896), (4096, 128), (896, 128),
        (32,), (256, 512), (256,),
    )
    if lax.axis_size(AXIS) == 16 and shapes == fits:
        return fused(*arrays)
    return on_device(*arrays)


def solution(mesh):
    placed = (
        P(("parts", "tensor"), None),
        P(("parts", "tensor"), None),
        P("parts", "tensor"),
        P("parts", "tensor"),
        P(),
        P("tensor", None),
        P("parts"),
        P("parts", "tensor"),
        P("parts"),
    )
    return jax.shard_map(
        choose,
        mesh=mesh,
        in_specs=placed,
        out_specs=(P("parts", "tensor"), P("parts", "tensor")),
        check_vma=False,
    )
```
